32 devices in a mesh: chan: 8 (over y, x, core), tm: 4 (over z).
Axes of the slice: x: 2, y: 2, z: 4, core: 2. Of those that a mesh axis runs over, the one named last changes fastest.
Arguments:
- samples: bfloat16 [256, 96, 4096], P('chan', 'tm'), may hold values from -6 to 6
- taps: float32 [16, 4096], replicated, may hold values from -1.5 to 1.5
- block_tile: int32 [120], replicated, may hold values from 0 to 7, as said below
- tile_slots: int32 [8], replicated, may hold values from 0 to 7, as said below
- kern_u: bfloat16 [16, 30720], replicated, may hold values from -1.1953125 to 1.1953125
- kern_v: bfloat16 [16, 30720], replicated, may hold values from -1.1953125 to 1.1953125
Outputs:
- uv_grid: float32 [8, 2048, 2, 256], P('tm', 'chan')
The draws below stay inside these ranges and needn't reach their ends.
Inputs may be any that keep to these rules, and one draw needn't show every extreme that they name: `block_tile`: A tile's owner is (its position in tile_slots) // 2. The blocks that fall in the tiles of one owner are at most 60; in every draw one owner has exactly 60. `tile_slots`: each tile number stands once.
All inputs are finite; a program needn't handle non-finite values.
Results may differ from the reference program's by a relative error of at most 0.0077.
Values may be sent and summed in bfloat16 or wider, within the bound.
A program may use at most 192 MiB of HBM per device.

```python
import math
import jax
import jax.numpy as jnp
import numpy as np
from jax import lax

S = 256
L = 4096
TAPS = 16
SBLK = 16
GRID = 16
TILES_DEV = 2
F = 2048
GROUP = 64
FRAMES = 96
NSB = 16
NBLK = 120
NBASE = 30720
NTILES = 8
CAP = 60


def routing_tables(key):
    keys = jax.random.split(jax.random.fold_in(key, 7), 5)
    owners = NTILES // TILES_DEV
    slot_tile = jax.random.permutation(keys[0], NTILES).astype(jnp.int32)
    heavy = jax.random.randint(keys[1], (), 0, owners).astype(jnp.int32)
    block_order = jax.random.permutation(keys[2], NBLK).astype(jnp.int32)
    rest_slots = jax.random.permutation(keys[3], (owners - 1) * CAP)[:NBLK - CAP].astype(jnp.int32)
    rest_rank = rest_slots // CAP
    rest_owner = rest_rank + (rest_rank >= heavy).astype(jnp.int32)
    owner_by_pos = jnp.concatenate([jnp.full((CAP,), heavy, jnp.int32), rest_owner])
    owner_of_block = jnp.zeros((NBLK,), jnp.int32).at[block_order].set(owner_by_pos)
    within = jax.random.randint(keys[4], (NBLK,), 0, TILES_DEV).astype(jnp.int32)
    block_tile = slot_tile[owner_of_block * TILES_DEV + within]
    return (block_tile.astype(jnp.int32), slot_tile)


def draw_block_tile(key, part):
    return routing_tables(key)[0]


def draw_tile_slots(key, part):
    return routing_tables(key)[1]


def block_levels(own_key, shape, cuts, low, top_value):
    level = 1.0
    for dim, blocks in cuts:
        draws = jax.random.uniform(jax.random.fold_in(jax.random.fold_in(own_key, 6), dim), (blocks,), jnp.float32, low / len(cuts), top_value / len(cuts))
        level = level * jnp.repeat(jnp.exp(draws), shape[dim] // blocks).reshape((-1,) + (1,) * (len(shape) - 1 - dim))
    return level


def centred(key, dims, deviation, limit, cuts=(), held_as=jnp.bfloat16):
    entries = jax.random.normal(key, dims, jnp.float32) * deviation
    if len(cuts) > 0:
        entries = block_levels(key, dims, cuts, -0.22, 0.18) * entries
    return jnp.clip(entries, min=-limit, max=limit).astype(held_as)


def setup_inputs(seed: int = 0) -> dict:
    key_of = jax.random.split(jax.random.key(seed), 7)
    samples = centred(key_of[0], (S, FRAMES, L), 1.0, 6.0, ((0, 8), (1, 4)))
    taps = centred(key_of[1], (TAPS, L), 0.25, 1.5, (), jnp.float32)
    block_tile = draw_block_tile(jax.random.fold_in(key_of[6], 71), 0)
    tile_slots = draw_tile_slots(jax.random.fold_in(key_of[6], 71), 0)
    kern_u = centred(key_of[4], (GRID, NBASE), 0.2, 1.1953125)
    kern_v = centred(key_of[5], (GRID, NBASE), 0.2, 1.1953125)
    return {"samples": samples, "taps": taps, "block_tile": block_tile, "tile_slots": tile_slots, "kern_u": kern_u, "kern_v": kern_v}


highest = lax.Precision.HIGHEST

def block_pairs(block_total):
    left_list = []
    right_list = []
    for p in range(block_total):
        for q in range(p + 1, block_total):
            left_list.append(p)
            right_list.append(q)
    return (np.array(left_list, dtype=np.int32), np.array(right_list, dtype=np.int32))

def reference(samples, taps, block_tile, tile_slots, kern_u, kern_v):
    positions = jnp.arange(L, dtype=jnp.int32)[:, None]
    channels = jnp.arange(F, dtype=jnp.int32)[None, :]
    phase_int = positions * channels % L
    phase_angle = phase_int.astype(jnp.float32) * (2.0 * math.pi / L)
    cosine = jnp.cos(phase_angle).astype(jnp.bfloat16)
    sine_neg = (-jnp.sin(phase_angle)).astype(jnp.bfloat16)
    dft_table = jnp.concatenate([cosine, sine_neg], axis=1).astype(jnp.float32)
    dft_scale = 1.0 / math.sqrt(L)

    def channelize(station_group):
        padded = jnp.concatenate([jnp.zeros((SBLK, TAPS - 1, L), station_group.dtype), station_group], axis=1)
        filtered = jnp.zeros((SBLK, FRAMES, L), jnp.float32)
        for tap_index in range(TAPS):
            offset = TAPS - 1 - tap_index
            filtered = filtered + taps[tap_index] * padded[:, offset:offset + FRAMES].astype(jnp.float32)
        rounded = lax.optimization_barrier(filtered.astype(jnp.bfloat16))
        rows_in = rounded.astype(jnp.float32).reshape(SBLK * FRAMES, L)
        spectrum = jnp.dot(rows_in, dft_table, precision=highest) * dft_scale
        return spectrum.astype(jnp.bfloat16).reshape(SBLK, FRAMES, 2, F)
    spectra = lax.map(channelize, samples.reshape(NSB, SBLK, FRAMES, L)).reshape(S, FRAMES, 2, F)
    left_idx, right_idx = block_pairs(NSB)
    u_cols = kern_u.astype(jnp.float32).reshape(GRID, NBLK, SBLK * SBLK).transpose(1, 2, 0)
    v_cols = kern_v.astype(jnp.float32).reshape(GRID, NBLK, SBLK * SBLK).transpose(1, 2, 0)
    kernel = (u_cols[:, :, :, None] * v_cols[:, :, None, :]).reshape(NBLK, SBLK * SBLK, GRID * GRID)
    kernel_wide = kernel.astype(jnp.bfloat16).astype(jnp.float32)
    tile_match = (block_tile[:, None] == tile_slots[None, :]).astype(jnp.float32)
    vis_scale = 1.0 / math.sqrt(FRAMES)

    def correlate(chan_start):
        chan_slice = lax.dynamic_slice_in_dim(spectra, chan_start, GROUP, axis=3).astype(jnp.float32)
        swapped = jnp.concatenate([chan_slice[:, :, 1:2], -chan_slice[:, :, 0:1]], axis=2)
        real_part = jnp.einsum('ibcg,jbcg->gij', chan_slice, chan_slice, precision=highest) * vis_scale
        imag_part = jnp.einsum('ibcg,jbcg->gij', swapped, chan_slice, precision=highest) * vis_scale
        visibility = jnp.stack([real_part, imag_part], axis=1).reshape(GROUP, 2, NSB, SBLK, NSB, SBLK)
        visibility = visibility[:, :, left_idx, :, right_idx, :]
        blocks = visibility.reshape(NBLK, GROUP, 2, SBLK * SBLK).astype(jnp.bfloat16).astype(jnp.float32)
        per_block = jnp.einsum('mgce,mel->mgcl', blocks, kernel_wide, precision=highest)
        return jnp.einsum('mgcl,ms->sgcl', per_block, tile_match, precision=highest)
    starts = jnp.arange(F // GROUP, dtype=jnp.int32) * GROUP
    tile_grids = lax.map(correlate, starts)
    return tile_grids.transpose(1, 0, 2, 3, 4).reshape(NTILES, F, 2, GRID * GRID)
```

```python
import functools
import math

import jax
import jax.numpy as jnp
import numpy as np
from jax import lax
from jax.experimental import pallas as pl
from jax.experimental.pallas import tpu as pltpu
from jax.sharding import PartitionSpec as P

SBLK = 16
GRID = 16
LANES = 128
HISTORY = 16
VMEM_LIMIT = 60 * 1024 * 1024


def passed_along(value, axis, steps):
    count = lax.axis_size(axis)
    leading, last = (max(0, -steps), min(count, count - steps))
    return lax.ppermute(value, axis, [(source, source + steps) for source in range(leading, last)])


def block_pairs(block_total):
    pairs = [(p, q) for p in range(block_total) for q in range(p + 1, block_total)]
    return np.array(pairs, dtype=np.int32)


def dft_tables(length, chan_size):
    half = length // 2
    channels = length // 2
    width = channels // chan_size // 2
    positions = np.arange(half, dtype=np.int64)[:, None, None]
    tables = []
    for parity in range(2):
        chans = (
            np.arange(chan_size, dtype=np.int64)[:, None] * 2 * width
            + 2 * np.arange(width, dtype=np.int64)[None, :]
            + parity
        )[None]
        angle = ((positions * chans) % length).astype(np.float64) * (2.0 * math.pi / length)
        table = np.stack([np.cos(angle), -np.sin(angle)], axis=2)
        tables.append(table.reshape(half, 2 * channels // 2).astype(jnp.bfloat16))
    return tables


def filter_kernel(lo_ref, hi_ref, hist_lo_ref, hist_hi_ref, taps_lo_ref, taps_hi_ref,
                  even_ref, odd_ref, wide):
    stations, frames, cols = lo_ref.shape
    tap_count = taps_lo_ref.shape[0]
    for side, (hist, body_ref) in enumerate(((hist_lo_ref, lo_ref), (hist_hi_ref, hi_ref))):
        wide[side, :HISTORY] = jnp.swapaxes(hist[...].astype(jnp.float32), 0, 1)
        wide[side, HISTORY:] = jnp.swapaxes(body_ref[...].astype(jnp.float32), 0, 1)
    span = 4
    rows = 16
    for lane in range(0, cols, LANES):
        lanes = slice(lane, lane + LANES)

        def step(index, carry):
            station = pl.multiple_of((index % (stations // rows)) * rows, rows)
            frame = (index // (stations // rows)) * span
            sums = []
            for side, taps_ref in enumerate((taps_lo_ref, taps_hi_ref)):
                values = [
                    wide[side, frame + HISTORY - (tap_count - 1) + k, pl.ds(station, rows), lanes]
                    for k in range(span + tap_count - 1)
                ]
                accs = [jnp.zeros((rows, LANES), jnp.float32) for _ in range(span)]
                for tap in range(tap_count):
                    weight = taps_ref[tap : tap + 1, lanes]
                    for b in range(span):
                        accs[b] = accs[b] + weight * values[b + tap_count - 1 - tap]
                sums.append(accs)
            for b in range(span):
                even_ref[frame + b, pl.ds(station, rows), lanes] = (
                    sums[0][b] + sums[1][b]
                ).astype(jnp.bfloat16)
                odd_ref[frame + b, pl.ds(station, rows), lanes] = (
                    sums[0][b] - sums[1][b]
                ).astype(jnp.bfloat16)
            return carry

        lax.fori_loop(0, (stations // rows) * (frames // span), step, 0)


def filtered_halves(samples, history, taps):
    stations, frames, length = samples.shape
    tap_count = taps.shape[0]
    half = length // 2
    cols = 256
    steps = half // cols
    lo = lambda j: (0, 0, j)
    hi = lambda j: (0, 0, j + steps)
    out = jax.ShapeDtypeStruct((frames, stations, half), jnp.bfloat16)
    out_spec = pl.BlockSpec((frames, stations, cols), lo)
    return pl.pallas_call(
        filter_kernel,
        grid=(steps,),
        in_specs=[
            pl.BlockSpec((stations, frames, cols), lo),
            pl.BlockSpec((stations, frames, cols), hi),
            pl.BlockSpec((stations, HISTORY, cols), lo),
            pl.BlockSpec((stations, HISTORY, cols), hi),
            pl.BlockSpec((tap_count, cols), lambda j: (0, j)),
            pl.BlockSpec((tap_count, cols), lambda j: (0, j + steps)),
        ],
        out_specs=[out_spec, out_spec],
        out_shape=[out, out],
        scratch_shapes=[pltpu.VMEM((2, HISTORY + frames, stations, cols), jnp.float32)],
        compiler_params=pltpu.CompilerParams(vmem_limit_bytes=VMEM_LIMIT),
        cost_estimate=pl.CostEstimate(
            flops=2 * tap_count * samples.size, bytes_accessed=5 * samples.size, transcendentals=0
        ),
    )(samples, samples, history, history, taps, taps)


def dft_kernel(scale, rows_ref, table_ref, out_ref):
    out_ref[0] = (
        jnp.dot(rows_ref[...], table_ref[...], preferred_element_type=jnp.float32) * scale
    ).astype(jnp.bfloat16)


def dft(rows, table, chan_size, scale):
    row_count, depth = rows.shape
    width = table.shape[1] // chan_size
    return pl.pallas_call(
        functools.partial(dft_kernel, scale),
        grid=(chan_size,),
        in_specs=[
            pl.BlockSpec((row_count, depth), lambda c: (0, 0)),
            pl.BlockSpec((depth, width), lambda c: (0, c)),
        ],
        out_specs=pl.BlockSpec((1, row_count, width), lambda c: (c, 0, 0)),
        out_shape=jax.ShapeDtypeStruct((chan_size, row_count, width), jnp.bfloat16),
        compiler_params=pltpu.CompilerParams(vmem_limit_bytes=VMEM_LIMIT),
        cost_estimate=pl.CostEstimate(
            flops=2 * rows.size * table.shape[1],
            bytes_accessed=2 * (rows.size + table.size + row_count * table.shape[1]),
            transcendentals=0,
        ),
    )(rows, table)


def weights_kernel(shift_ref, u_ref, v_ref, out_ref):
    per_step, rows, cells = out_ref.shape
    first = pl.program_id(0) * per_step
    u_of = lax.broadcasted_iota(jnp.int32, (GRID, cells), 1) // GRID
    v_of = lax.broadcasted_iota(jnp.int32, (GRID, cells), 1) % GRID
    grid_row = lax.broadcasted_iota(jnp.int32, (GRID, cells), 0)
    spread_u = (u_of == grid_row).astype(jnp.bfloat16)
    spread_v = (v_of == grid_row).astype(jnp.bfloat16)
    dims = (((0,), (0,)), ((), ()))
    for k in range(per_step):
        shift = shift_ref[first + k]
        for part in range(rows // LANES):
            where = pl.ds(k * rows + part * LANES, LANES)
            u_part = pltpu.roll(u_ref[:, where].astype(jnp.float32), shift, 1).astype(jnp.bfloat16)
            v_part = pltpu.roll(v_ref[:, where].astype(jnp.float32), shift, 1).astype(jnp.bfloat16)
            u_wide = lax.dot_general(u_part, spread_u, dims, preferred_element_type=jnp.float32)
            v_wide = lax.dot_general(v_part, spread_v, dims, preferred_element_type=jnp.float32)
            out_ref[k, part * LANES : (part + 1) * LANES, :] = (u_wide * v_wide).astype(
                jnp.bfloat16
            )


def grid_weights(kern_u, kern_v, shifts):
    rows = SBLK * SBLK
    blocks = kern_u.shape[1] // rows
    per_step = 8
    spec = pl.BlockSpec((GRID, per_step * rows), lambda m, shift: (0, m))
    return pl.pallas_call(
        weights_kernel,
        grid_spec=pltpu.PrefetchScalarGridSpec(
            num_scalar_prefetch=1,
            grid=(blocks // per_step,),
            in_specs=[spec, spec],
            out_specs=pl.BlockSpec((per_step, rows, GRID * GRID), lambda m, shift: (m, 0, 0)),
        ),
        out_shape=jax.ShapeDtypeStruct((blocks, rows, GRID * GRID), jnp.bfloat16),
        compiler_params=pltpu.CompilerParams(vmem_limit_bytes=VMEM_LIMIT),
    )(shifts, kern_u, kern_v)


def correlate_kernel(scale, slot_ref, turned_ref, weights_ref, out_ref, spectra, vis, blocks):
    sources, frames, source_stations, width = turned_ref.shape
    stations = sources * source_stations
    group = width // 2
    tiles, chunks, rows, cells = out_ref.shape
    per_chunk = rows // 2
    half = stations // 2
    half_blocks = half // SBLK
    block_rows = stations // SBLK
    pieces = LANES // SBLK

    out_ref[...] = jnp.zeros_like(out_ref)

    def turn(frame, carry):
        values = turned_ref[:, frame].astype(jnp.float32).reshape(stations, width)
        flipped = values.T
        where = pl.ds(pl.multiple_of(frame * width, width), width)
        for side in range(2):
            spectra[side, where, :] = flipped[:, side * LANES : (side + 1) * LANES]
        return carry

    lax.fori_loop(0, frames, turn, 0)

    lane_piece = lax.broadcasted_iota(jnp.int32, (16, LANES), 1) // SBLK
    masks = [(lane_piece & (1 << bit)) != 0 for bit in range(3)]

    def chunk_step(chunk, carry):
        for phase in range(2):
            sides = (0, 1) if phase == 0 else (1,)

            def channel(index, inner):
                channel_index = chunk * per_chunk + index
                real = [
                    spectra.at[s][pl.ds(channel_index, frames, stride=width), :] for s in range(2)
                ]
                imag = [
                    spectra.at[s][pl.ds(group + channel_index, frames, stride=width), :]
                    for s in range(2)
                ]
                right = jnp.concatenate(
                    [jnp.concatenate([real[s], imag[s]], axis=0) for s in sides], axis=1
                ).astype(jnp.bfloat16)
                left = jnp.concatenate(
                    [
                        jnp.concatenate([real[phase], imag[phase]], axis=0),
                        jnp.concatenate([imag[phase], -real[phase]], axis=0),
                    ],
                    axis=1,
                ).astype(jnp.bfloat16)
                product = (
                    lax.dot_general(
                        left, right, (((0,), (0,)), ((), ())), preferred_element_type=jnp.float32
                    )
                    * scale
                )
                for part in range(2):
                    for place, side in enumerate(sides):
                        vis.at[side][pl.ds(part * per_chunk + index, half, stride=rows), :] = (
                            product[
                                part * half : (part + 1) * half,
                                place * LANES : (place + 1) * LANES,
                            ]
                        )
                return inner

            lax.fori_loop(0, per_chunk, channel, 0)

            def block_row(local, inner):
                p = phase * half_blocks + local
                for side in sides:
                    def rearrange(tile, innermost):
                        row = pl.multiple_of(tile * 16, 16)
                        for upper in range(2):
                            turned = []
                            for a in range(pieces):
                                start = pl.multiple_of(
                                    (local * SBLK + upper * pieces + a) * rows, rows
                                )
                                value = vis[side, pl.ds(start + row, 16), :]
                                if a:
                                    value = pltpu.roll(value, a * SBLK, 1)
                                turned.append(value)
                            for bit in range(3):
                                turned = [
                                    jnp.where(
                                        masks[bit], turned[(x + (1 << bit)) % pieces], turned[x]
                                    )
                                    for x in range(pieces)
                                ]
                            for piece in range(pieces):
                                blocks[
                                    piece,
                                    pl.ds(row, 16),
                                    upper * LANES : (upper + 1) * LANES,
                                ] = turned[-piece % pieces].astype(jnp.bfloat16)
                        return innermost

                    lax.fori_loop(0, rows // 16, rearrange, 0)
                    for piece in range(pieces):
                        q = side * pieces + piece

                        @pl.when(q > p)
                        def _():
                            m = p * (2 * block_rows - p - 1) // 2 + q - p - 1
                            slot = slot_ref[m]
                            out_ref[slot, chunk] += jnp.dot(
                                blocks[piece],
                                weights_ref[m],
                                preferred_element_type=jnp.float32,
                            )
                return inner

            lax.fori_loop(0, half_blocks, block_row, 0)
        return carry

    lax.fori_loop(0, chunks, chunk_step, 0)


def gridded(turned, weights, slot_of_block, tile_count, total_frames):
    sources, frames, source_stations, width = turned.shape
    stations = sources * source_stations
    group = width // 2
    per_chunk = min(group, 64)
    chunks = group // per_chunk
    rows = 2 * per_chunk
    cells = GRID * GRID
    whole = pl.BlockSpec(memory_space=pltpu.VMEM)
    return pl.pallas_call(
        functools.partial(correlate_kernel, 1.0 / math.sqrt(total_frames)),
        in_specs=[pl.BlockSpec(memory_space=pltpu.SMEM), whole, whole],
        out_specs=whole,
        out_shape=jax.ShapeDtypeStruct((tile_count, chunks, rows, cells), jnp.float32),
        scratch_shapes=[
            pltpu.VMEM((2, frames * width, LANES), jnp.float32),
            pltpu.VMEM((2, stations // 2 * rows, LANES), jnp.float32),
            pltpu.VMEM((LANES // SBLK, rows, SBLK * SBLK), jnp.bfloat16),
        ],
        compiler_params=pltpu.CompilerParams(vmem_limit_bytes=VMEM_LIMIT),
        cost_estimate=pl.CostEstimate(
            flops=2 * weights.size * rows * chunks,
            bytes_accessed=2 * (weights.size + turned.size),
            transcendentals=0,
        ),
    )(slot_of_block, turned, weights)


def body(samples, taps, block_tile, tile_slots, kern_u, kern_v):
    station_count, frame_count, length = samples.shape
    chan_size = lax.axis_size("chan")
    tm_size = lax.axis_size("tm")
    half = length // 2
    history = passed_along(samples[:, frame_count - HISTORY :], "tm", 1)
    halves = filtered_halves(samples, history, taps)
    tables = dft_tables(length, chan_size)
    dft_scale = 1.0 / math.sqrt(length)

    tile_count = tile_slots.shape[0]
    slot_ids = jnp.arange(tile_count, dtype=jnp.int32)
    tile_match = block_tile[:, None] == tile_slots[None, :]
    slot_of_block = jnp.sum(jnp.where(tile_match, slot_ids[None, :], 0), axis=1).astype(jnp.int32)
    pairs = block_pairs(station_count * chan_size // SBLK)
    pieces = LANES // SBLK
    shifts = jnp.asarray((pairs[:, 1] % pieces) * SBLK, jnp.int32)
    weights = grid_weights(kern_u, kern_v, shifts)

    grids = []
    for parity in range(2):
        rows_in = halves[parity].reshape(frame_count * station_count, half)
        spectrum = dft(rows_in, jnp.asarray(tables[parity]), chan_size, dft_scale)
        turned = lax.all_to_all(spectrum, "chan", split_axis=0, concat_axis=0, tiled=True)
        turned = turned.reshape(chan_size, frame_count, station_count, spectrum.shape[-1])
        partial_grid = gridded(
            turned, weights, slot_of_block, tile_count, frame_count * tm_size
        )
        owned = lax.psum_scatter(partial_grid, "tm", scatter_dimension=0, tiled=True)
        owned_tiles, chunks, rows, cells = owned.shape
        owned = owned.reshape(owned_tiles, chunks, 2, rows // 2, cells).transpose(0, 1, 3, 2, 4)
        grids.append(owned.reshape(owned_tiles, chunks * rows // 2, 1, 2, cells))
    uv_grid = jnp.concatenate(grids, axis=2)
    return uv_grid.reshape(uv_grid.shape[0], -1, 2, uv_grid.shape[-1])


def solution(mesh):
    placed = (P("chan", "tm", None), P(), P(), P(), P(), P())
    return jax.shard_map(
        body, mesh=mesh, in_specs=placed, out_specs=P("tm", "chan", None, None), check_vma=False
    )
```

```python
import functools
import math

import jax
import jax.numpy as jnp
import numpy as np
from jax import lax
from jax.experimental import pallas as pl
from jax.experimental.pallas import tpu as pltpu
from jax.sharding import PartitionSpec as P

SBLK = 16
GRID = 16
LANES = 128
HISTORY = 16
VMEM_LIMIT = 60 * 1024 * 1024


def passed_along(value, axis, steps):
    count = lax.axis_size(axis)
    leading, last = (max(0, -steps), min(count, count - steps))
    return lax.ppermute(value, axis, [(source, source + steps) for source in range(leading, last)])


def block_pairs(block_total):
    pairs = [(p, q) for p in range(block_total) for q in range(p + 1, block_total)]
    return np.array(pairs, dtype=np.int32)


def dft_tables(length, chan_size):
    half = length // 2
    channels = length // 2
    width = channels // chan_size // 2
    positions = np.arange(half, dtype=np.int64)[:, None, None]
    tables = []
    for parity in range(2):
        chans = (
            np.arange(chan_size, dtype=np.int64)[:, None] * 2 * width
            + 2 * np.arange(width, dtype=np.int64)[None, :]
            + parity
        )[None]
        angle = ((positions * chans) % length).astype(np.float64) * (2.0 * math.pi / length)
        table = np.stack([np.cos(angle), -np.sin(angle)], axis=2)
        tables.append(table.reshape(half, 2 * channels // 2).astype(jnp.bfloat16))
    return tables


def filter_kernel(early, *refs):
    if early:
        hist_lo, hist_hi, lo_ref, hi_ref, taps_lo_ref, taps_hi_ref, even_ref, odd_ref, wide = refs
        parts = ((hist_lo, lo_ref), (hist_hi, hi_ref))
    else:
        lo_ref, hi_ref, taps_lo_ref, taps_hi_ref, even_ref, odd_ref, wide = refs
        parts = ((lo_ref,), (hi_ref,))
    frames, stations, cols = even_ref.shape
    tap_count = taps_lo_ref.shape[0]
    for side, sources in enumerate(parts):
        if early:
            wide[side, :HISTORY] = jnp.swapaxes(sources[0][...].astype(jnp.float32), 0, 1)
            whole = jnp.swapaxes(sources[1][...].astype(jnp.float32), 0, 1)
            wide[side, HISTORY:] = whole[:frames]
        else:
            wide[side] = jnp.swapaxes(sources[0][...].astype(jnp.float32), 0, 1)
    span = 4
    rows = 16
    for lane in range(0, cols, LANES):
        lanes = slice(lane, lane + LANES)

        def step(index, carry):
            station = pl.multiple_of((index % (stations // rows)) * rows, rows)
            frame = (index // (stations // rows)) * span
            sums = []
            for side, taps_ref in enumerate((taps_lo_ref, taps_hi_ref)):
                values = [
                    wide[side, frame + HISTORY - (tap_count - 1) + k, pl.ds(station, rows), lanes]
                    for k in range(span + tap_count - 1)
                ]
                accs = [jnp.zeros((rows, LANES), jnp.float32) for _ in range(span)]
                for tap in range(tap_count):
                    weight = taps_ref[tap : tap + 1, lanes]
                    for b in range(span):
                        accs[b] = accs[b] + weight * values[b + tap_count - 1 - tap]
                sums.append(accs)
            for b in range(span):
                even_ref[frame + b, pl.ds(station, rows), lanes] = (
                    sums[0][b] + sums[1][b]
                ).astype(jnp.bfloat16)
                odd_ref[frame + b, pl.ds(station, rows), lanes] = (
                    sums[0][b] - sums[1][b]
                ).astype(jnp.bfloat16)
            return carry

        lax.fori_loop(0, (stations // rows) * (frames // span), step, 0)


def filtered_halves(samples, history, taps):
    stations, all_frames, length = samples.shape
    early = history is not None
    frames = HISTORY if early else all_frames - HISTORY
    tap_count = taps.shape[0]
    half = length // 2
    cols = 256
    steps = half // cols
    lo = lambda j: (0, 0, j)
    hi = lambda j: (0, 0, j + steps)
    out = jax.ShapeDtypeStruct((frames, stations, half), jnp.bfloat16)
    out_spec = pl.BlockSpec((frames, stations, cols), lo)
    operands = [samples, samples, taps, taps]
    specs = [
        pl.BlockSpec((stations, all_frames, cols), lo),
        pl.BlockSpec((stations, all_frames, cols), hi),
        pl.BlockSpec((tap_count, cols), lambda j: (0, j)),
        pl.BlockSpec((tap_count, cols), lambda j: (0, j + steps)),
    ]
    if early:
        operands = [history, history] + operands
        specs = [
            pl.BlockSpec((stations, HISTORY, cols), lo),
            pl.BlockSpec((stations, HISTORY, cols), hi),
        ] + specs
    return pl.pallas_call(
        functools.partial(filter_kernel, early),
        grid=(steps,),
        in_specs=specs,
        out_specs=[out_spec, out_spec],
        out_shape=[out, out],
        scratch_shapes=[pltpu.VMEM((2, HISTORY + frames, stations, cols), jnp.float32)],
        compiler_params=pltpu.CompilerParams(vmem_limit_bytes=VMEM_LIMIT),
        cost_estimate=pl.CostEstimate(
            flops=2 * tap_count * stations * frames * length,
            bytes_accessed=4 * samples.size,
            transcendentals=0,
        ),
    )(*operands)


def dft_kernel(scale, me_ref, rows_ref, table_ref, out_ref):
    out_ref[0] = (
        jnp.dot(rows_ref[...], table_ref[...], preferred_element_type=jnp.float32) * scale
    ).astype(jnp.bfloat16)


def dft(rows, table, chan_size, scale, me):
    row_count, depth = rows.shape
    width = table.shape[1] // chan_size
    return pl.pallas_call(
        functools.partial(dft_kernel, scale),
        grid_spec=pltpu.PrefetchScalarGridSpec(
            num_scalar_prefetch=1,
            grid=(chan_size,),
            in_specs=[
                pl.BlockSpec((row_count, depth), lambda k, me: (0, 0)),
                pl.BlockSpec((depth, width), lambda k, me: (0, me[0] ^ k)),
            ],
            out_specs=pl.BlockSpec((1, row_count, width), lambda k, me: (k, 0, 0)),
        ),
        out_shape=jax.ShapeDtypeStruct((chan_size, row_count, width), jnp.bfloat16),
        compiler_params=pltpu.CompilerParams(vmem_limit_bytes=VMEM_LIMIT),
        cost_estimate=pl.CostEstimate(
            flops=2 * rows.size * table.shape[1],
            bytes_accessed=2 * (rows.size + table.size + row_count * table.shape[1]),
            transcendentals=0,
        ),
    )(me, rows, table)


def exchanged(blocks, shape):
    count = blocks.shape[0]
    pieces = []
    for k in range(count):
        piece = blocks[k].reshape(shape)
        if k:
            piece = lax.ppermute(piece, "chan", [(c, c ^ k) for c in range(count)])
        pieces.append(piece)
    return pieces


def weights_kernel(shift_ref, u_ref, v_ref, out_ref):
    per_step, rows, cells = out_ref.shape
    first = pl.program_id(0) * per_step
    u_of = lax.broadcasted_iota(jnp.int32, (GRID, cells), 1) // GRID
    v_of = lax.broadcasted_iota(jnp.int32, (GRID, cells), 1) % GRID
    grid_row = lax.broadcasted_iota(jnp.int32, (GRID, cells), 0)
    spread_u = (u_of == grid_row).astype(jnp.bfloat16)
    spread_v = (v_of == grid_row).astype(jnp.bfloat16)
    dims = (((0,), (0,)), ((), ()))
    for k in range(per_step):
        shift = shift_ref[first + k]
        for part in range(rows // LANES):
            where = pl.ds(k * rows + part * LANES, LANES)
            u_part = pltpu.roll(u_ref[:, where].astype(jnp.float32), shift, 1).astype(jnp.bfloat16)
            v_part = pltpu.roll(v_ref[:, where].astype(jnp.float32), shift, 1).astype(jnp.bfloat16)
            u_wide = lax.dot_general(u_part, spread_u, dims, preferred_element_type=jnp.float32)
            v_wide = lax.dot_general(v_part, spread_v, dims, preferred_element_type=jnp.float32)
            out_ref[k, part * LANES : (part + 1) * LANES, :] = (u_wide * v_wide).astype(
                jnp.bfloat16
            )


def grid_weights(kern_u, kern_v, shifts):
    rows = SBLK * SBLK
    blocks = kern_u.shape[1] // rows
    per_step = 8
    spec = pl.BlockSpec((GRID, per_step * rows), lambda m, shift: (0, m))
    return pl.pallas_call(
        weights_kernel,
        grid_spec=pltpu.PrefetchScalarGridSpec(
            num_scalar_prefetch=1,
            grid=(blocks // per_step,),
            in_specs=[spec, spec],
            out_specs=pl.BlockSpec((per_step, rows, GRID * GRID), lambda m, shift: (m, 0, 0)),
        ),
        out_shape=jax.ShapeDtypeStruct((blocks, rows, GRID * GRID), jnp.bfloat16),
        compiler_params=pltpu.CompilerParams(vmem_limit_bytes=VMEM_LIMIT),
    )(shifts, kern_u, kern_v)


def correlate_kernel(
    scale, sources, parity, slot_ref, me_ref, *refs
):
    early_refs, late_refs = refs[:sources], refs[sources : 2 * sources]
    weights_hbm, out_ref = refs[2 * sources : 2 * sources + 2]
    staged, spectra, vis, blocks_a, blocks_b, acc, weights_ref, weights_sem = refs[
        2 * sources + 2 :
    ]
    early_frames, source_stations, width = early_refs[0].shape
    late_frames = late_refs[0].shape[0]
    frames = early_frames + late_frames
    stations = sources * source_stations
    group = width // 2
    tiles, rows, cells = out_ref.shape
    block_rows = stations // SBLK
    pieces = LANES // SBLK
    strip = LANES // 2
    strip_blocks = strip // SBLK
    pitch = rows + 1
    unroll = 4

    copy = pltpu.make_async_copy(weights_hbm, weights_ref, weights_sem)
    copy.start()
    acc[...] = jnp.zeros_like(acc)

    def turn(frame, source_refs, lanes, place):
        for k in range(sources):
            start = pl.multiple_of((me_ref[0] ^ k) * source_stations, source_stations)
            staged[pl.ds(start, source_stations), :] = source_refs[k][frame, :, lanes].astype(
                jnp.float32
            )
        flipped = staged[...].T
        for side in range(2):
            spectra[side, pl.ds(place * pitch, width), :] = flipped[
                :, side * LANES : (side + 1) * LANES
            ]

    def turn_early(frame, carry):
        turn(frame, early_refs, slice(None), frame)
        return carry

    def turn_late(frame, carry):
        turn(frame, late_refs, slice(parity * width, (parity + 1) * width), frame + early_frames)
        return carry

    lax.fori_loop(0, early_frames, turn_early, 0)
    lax.fori_loop(0, late_frames, turn_late, 0)

    lane_piece = lax.broadcasted_iota(jnp.int32, (16, LANES), 1) // SBLK
    masks = [(lane_piece & (1 << bit)) != 0 for bit in range(3)]

    for index in range(stations // strip):
        own_side = index * strip // LANES
        offset = index * strip % LANES
        sides = tuple(range(own_side, 2))

        def channels(step, carry):
            for inner in range(unroll):
                channel = step * unroll + inner
                real = [
                    spectra.at[s][pl.ds(channel, frames, stride=pitch), :] for s in range(2)
                ]
                imag = [
                    spectra.at[s][pl.ds(group + channel, frames, stride=pitch), :]
                    for s in range(2)
                ]
                right = jnp.concatenate(
                    [jnp.concatenate([real[s], imag[s]], axis=0) for s in sides], axis=1
                ).astype(jnp.bfloat16)
                own_real = real[own_side][:, offset : offset + strip]
                own_imag = imag[own_side][:, offset : offset + strip]
                left = jnp.concatenate(
                    [
                        jnp.concatenate([own_real, own_imag], axis=1),
                        jnp.concatenate([own_imag, -own_real], axis=1),
                    ],
                    axis=0,
                ).astype(jnp.bfloat16)
                product = lax.dot_general(
                    left, right, (((0,), (0,)), ((), ())), preferred_element_type=jnp.float32
                )
                for part in range(2):
                    for place, side in enumerate(sides):
                        vis.at[side][pl.ds(part * group + channel, strip, stride=pitch), :] = (
                            product[
                                part * strip : (part + 1) * strip,
                                place * LANES : (place + 1) * LANES,
                            ]
                        )
            return carry

        lax.fori_loop(0, group // unroll, channels, 0)
        if index == 0:
            copy.wait()

        def rearrange(step, tile, target):
            side = own_side + step // strip_blocks
            local = step % strip_blocks
            row = pl.multiple_of(tile * 16, 16)
            for upper in range(2):
                turned = []
                for a in range(pieces):
                    start = (local * SBLK + upper * pieces + a) * pitch + row
                    value = vis[side, pl.ds(start, 16), :]
                    if a:
                        value = pltpu.roll(value, a * SBLK, 1)
                    turned.append(value)
                for bit in range(3):
                    turned = [
                        jnp.where(masks[bit], turned[(x + (1 << bit)) % pieces], turned[x])
                        for x in range(pieces)
                    ]
                for piece in range(pieces):
                    target[piece, pl.ds(row, 16), upper * LANES : (upper + 1) * LANES] = turned[
                        -piece % pieces
                    ].astype(jnp.bfloat16)

        steps = strip_blocks * len(sides)
        per_piece = rows // 16 // pieces

        def first(tile, carry):
            rearrange(0, tile, blocks_a)
            return carry

        lax.fori_loop(0, rows // 16, first, 0)

        def pair_step(pair, carry):
            for odd, (current, following) in enumerate(
                ((blocks_a, blocks_b), (blocks_b, blocks_a))
            ):
                step = 2 * pair + odd
                p = index * strip_blocks + step % strip_blocks
                side = own_side + step // strip_blocks
                next_step = jnp.minimum(step + 1, steps - 1)

                def one_piece(piece, inner):
                    q = side * pieces + piece
                    valid = q > p
                    m = jnp.where(valid, p * (2 * block_rows - p - 1) // 2 + q - p - 1, 0)
                    slot = jnp.where(valid, slot_ref[m], tiles)
                    product = jnp.dot(
                        current[piece], weights_ref[m], preferred_element_type=jnp.float32
                    )
                    for tile in range(per_piece):
                        rearrange(next_step, piece * per_piece + tile, following)
                    acc[slot] += product
                    return inner

                lax.fori_loop(0, pieces, one_piece, 0)
            return carry

        lax.fori_loop(0, steps // 2, pair_step, 0)

    for tile in range(tiles):
        out_ref[tile] = acc[tile] * scale


def gridded(early, late, parity, weights, slot_of_block, me, tile_count, total_frames):
    sources = len(early)
    early_frames, source_stations, width = early[0].shape
    frames = early_frames + late[0].shape[0]
    stations = sources * source_stations
    cells = GRID * GRID
    pitch = width + 1
    whole = pl.BlockSpec(memory_space=pltpu.VMEM)
    scalars = pl.BlockSpec(memory_space=pltpu.SMEM)
    block = pltpu.VMEM((LANES // SBLK, width, SBLK * SBLK), jnp.bfloat16)
    return pl.pallas_call(
        functools.partial(correlate_kernel, 1.0 / math.sqrt(total_frames), sources, parity),
        in_specs=[scalars, scalars] + [whole] * (2 * sources) + [pl.BlockSpec(memory_space=pl.ANY)],
        out_specs=whole,
        out_shape=jax.ShapeDtypeStruct((tile_count, width, cells), jnp.float32),
        scratch_shapes=[
            pltpu.VMEM((stations, width), jnp.float32),
            pltpu.VMEM((2, -(-frames * pitch // 8) * 8, LANES), jnp.float32),
            pltpu.VMEM((2, LANES // 2 * pitch, LANES), jnp.float32),
            block,
            block,
            pltpu.VMEM((tile_count + 1, width, cells), jnp.float32),
            pltpu.VMEM(weights.shape, weights.dtype),
            pltpu.SemaphoreType.DMA,
        ],
        compiler_params=pltpu.CompilerParams(vmem_limit_bytes=VMEM_LIMIT),
        cost_estimate=pl.CostEstimate(
            flops=8 * weights.size * width,
            bytes_accessed=2 * weights.size,
            transcendentals=0,
        ),
    )(slot_of_block, me, *early, *late, weights)


def body(samples, taps, block_tile, tile_slots, kern_u, kern_v):
    station_count, frame_count, length = samples.shape
    chan_size = lax.axis_size("chan")
    tm_size = lax.axis_size("tm")
    half = length // 2
    history = passed_along(samples[:, frame_count - HISTORY :], "tm", 1)
    me = lax.axis_index("chan").astype(jnp.int32).reshape(1)
    tables = [jnp.asarray(table) for table in dft_tables(length, chan_size)]
    dft_scale = 1.0 / math.sqrt(length)

    tile_count = tile_slots.shape[0]
    slot_ids = jnp.arange(tile_count, dtype=jnp.int32)
    tile_match = block_tile[:, None] == tile_slots[None, :]
    slot_of_block = jnp.sum(jnp.where(tile_match, slot_ids[None, :], 0), axis=1).astype(jnp.int32)
    pairs = block_pairs(station_count * chan_size // SBLK)
    pieces = LANES // SBLK
    shifts = jnp.asarray((pairs[:, 1] % pieces) * SBLK, jnp.int32)
    weights = grid_weights(kern_u, kern_v, shifts)

    def spectra_of(rows_in, parity):
        rows_in = rows_in.reshape(rows_in.shape[0] * station_count, half)
        return dft(rows_in, tables[parity], chan_size, dft_scale, me)

    late_rows = filtered_halves(samples, None, taps)
    late_blocks = jnp.concatenate([spectra_of(late_rows[0], 0), spectra_of(late_rows[1], 1)], axis=2)
    late = exchanged(late_blocks, (frame_count - HISTORY, station_count, late_blocks.shape[2]))
    early_rows = filtered_halves(samples, history, taps)

    grids = []
    for parity in range(2):
        early_blocks = spectra_of(early_rows[parity], parity)
        early = exchanged(early_blocks, (HISTORY, station_count, early_blocks.shape[2]))
        partial_grid = gridded(
            early, late, parity, weights, slot_of_block, me, tile_count, frame_count * tm_size
        )
        owned = lax.psum_scatter(partial_grid, "tm", scatter_dimension=0, tiled=True)
        owned_tiles, rows, cells = owned.shape
        owned = owned.reshape(owned_tiles, 2, rows // 2, cells).transpose(0, 2, 1, 3)
        grids.append(owned[:, :, None])
    uv_grid = jnp.concatenate(grids, axis=2)
    return uv_grid.reshape(uv_grid.shape[0], -1, 2, uv_grid.shape[-1])


def solution(mesh):
    placed = (P("chan", "tm", None), P(), P(), P(), P(), P())
    return jax.shard_map(
        body, mesh=mesh, in_specs=placed, out_specs=P("tm", "chan", None, None), check_vma=False
    )
```

```python
import functools
import math

import jax
import jax.numpy as jnp
import numpy as np
from jax import lax
from jax.experimental import pallas as pl
from jax.experimental.pallas import tpu as pltpu
from jax.sharding import PartitionSpec as P

SBLK = 16
GRID = 16
LANES = 128
HISTORY = 16
VMEM_LIMIT = 60 * 1024 * 1024


def passed_along(value, axis, steps):
    count = lax.axis_size(axis)
    leading, last = (max(0, -steps), min(count, count - steps))
    return lax.ppermute(value, axis, [(source, source + steps) for source in range(leading, last)])


def block_pairs(block_total):
    pairs = [(p, q) for p in range(block_total) for q in range(p + 1, block_total)]
    return np.array(pairs, dtype=np.int32)


def dft_tables(length, chan_size):
    half = length // 2
    channels = length // 2
    width = channels // chan_size // 2
    positions = np.arange(half, dtype=np.int64)[:, None, None]
    tables = []
    for parity in range(2):
        chans = (
            np.arange(chan_size, dtype=np.int64)[:, None] * 2 * width
            + 2 * np.arange(width, dtype=np.int64)[None, :]
            + parity
        )[None]
        angle = ((positions * chans) % length).astype(np.float64) * (2.0 * math.pi / length)
        table = np.stack([np.cos(angle), -np.sin(angle)], axis=2)
        tables.append(table.reshape(half, 2 * channels // 2).astype(jnp.bfloat16))
    return tables


def filter_kernel(early, *refs):
    if early:
        hist_lo, hist_hi, lo_ref, hi_ref, taps_lo_ref, taps_hi_ref, even_ref, odd_ref, wide = refs
        parts = ((hist_lo, lo_ref), (hist_hi, hi_ref))
    else:
        lo_ref, hi_ref, taps_lo_ref, taps_hi_ref, even_ref, odd_ref, wide = refs
        parts = ((lo_ref,), (hi_ref,))
    frames, stations, cols = even_ref.shape
    tap_count = taps_lo_ref.shape[0]
    for side, sources in enumerate(parts):
        if early:
            wide[side, :HISTORY] = jnp.swapaxes(sources[0][...].astype(jnp.float32), 0, 1)
            whole = jnp.swapaxes(sources[1][...].astype(jnp.float32), 0, 1)
            wide[side, HISTORY:] = whole[:frames]
        else:
            wide[side] = jnp.swapaxes(sources[0][...].astype(jnp.float32), 0, 1)
    span = 4
    rows = 16
    for lane in range(0, cols, LANES):
        lanes = slice(lane, lane + LANES)

        def step(index, carry):
            station = pl.multiple_of((index % (stations // rows)) * rows, rows)
            frame = (index // (stations // rows)) * span
            sums = []
            for side, taps_ref in enumerate((taps_lo_ref, taps_hi_ref)):
                values = [
                    wide[side, frame + HISTORY - (tap_count - 1) + k, pl.ds(station, rows), lanes]
                    for k in range(span + tap_count - 1)
                ]
                accs = [jnp.zeros((rows, LANES), jnp.float32) for _ in range(span)]
                for tap in range(tap_count):
                    weight = taps_ref[tap : tap + 1, lanes]
                    for b in range(span):
                        accs[b] = accs[b] + weight * values[b + tap_count - 1 - tap]
                sums.append(accs)
            for b in range(span):
                even_ref[frame + b, pl.ds(station, rows), lanes] = (
                    sums[0][b] + sums[1][b]
                ).astype(jnp.bfloat16)
                odd_ref[frame + b, pl.ds(station, rows), lanes] = (
                    sums[0][b] - sums[1][b]
                ).astype(jnp.bfloat16)
            return carry

        lax.fori_loop(0, (stations // rows) * (frames // span), step, 0)


def filtered_halves(samples, history, taps):
    stations, all_frames, length = samples.shape
    early = history is not None
    frames = HISTORY if early else all_frames - HISTORY
    tap_count = taps.shape[0]
    half = length // 2
    cols = 256
    steps = half // cols
    lo = lambda j: (0, 0, j)
    hi = lambda j: (0, 0, j + steps)
    out = jax.ShapeDtypeStruct((frames, stations, half), jnp.bfloat16)
    out_spec = pl.BlockSpec((frames, stations, cols), lo)
    operands = [samples, samples, taps, taps]
    specs = [
        pl.BlockSpec((stations, all_frames, cols), lo),
        pl.BlockSpec((stations, all_frames, cols), hi),
        pl.BlockSpec((tap_count, cols), lambda j: (0, j)),
        pl.BlockSpec((tap_count, cols), lambda j: (0, j + steps)),
    ]
    if early:
        operands = [history, history] + operands
        specs = [
            pl.BlockSpec((stations, HISTORY, cols), lo),
            pl.BlockSpec((stations, HISTORY, cols), hi),
        ] + specs
    return pl.pallas_call(
        functools.partial(filter_kernel, early),
        grid=(steps,),
        in_specs=specs,
        out_specs=[out_spec, out_spec],
        out_shape=[out, out],
        scratch_shapes=[pltpu.VMEM((2, HISTORY + frames, stations, cols), jnp.float32)],
        compiler_params=pltpu.CompilerParams(vmem_limit_bytes=VMEM_LIMIT),
        cost_estimate=pl.CostEstimate(
            flops=640 * tap_count * stations * frames * length,
            bytes_accessed=4 * samples.size,
            transcendentals=0,
        ),
    )(*operands)


def dft_kernel(scale, me_ref, rows_ref, table_ref, out_ref):
    out_ref[0] = (
        jnp.dot(rows_ref[...], table_ref[...], preferred_element_type=jnp.float32) * scale
    ).astype(jnp.bfloat16)


def dft(rows, table, chan_size, scale, me):
    row_count, depth = rows.shape
    width = table.shape[1] // chan_size
    return pl.pallas_call(
        functools.partial(dft_kernel, scale),
        grid_spec=pltpu.PrefetchScalarGridSpec(
            num_scalar_prefetch=1,
            grid=(chan_size,),
            in_specs=[
                pl.BlockSpec((row_count, depth), lambda k, me: (0, 0)),
                pl.BlockSpec((depth, width), lambda k, me: (0, me[0] ^ k)),
            ],
            out_specs=pl.BlockSpec((1, row_count, width), lambda k, me: (k, 0, 0)),
        ),
        out_shape=jax.ShapeDtypeStruct((chan_size, row_count, width), jnp.bfloat16),
        compiler_params=pltpu.CompilerParams(vmem_limit_bytes=VMEM_LIMIT),
        cost_estimate=pl.CostEstimate(
            flops=2 * rows.size * table.shape[1],
            bytes_accessed=2 * (rows.size + table.size + row_count * table.shape[1]),
            transcendentals=0,
        ),
    )(me, rows, table)


def exchanged(blocks, shape):
    count = blocks.shape[0]
    pieces = []
    for k in range(count):
        piece = blocks[k].reshape(shape)
        if k:
            piece = lax.ppermute(piece, "chan", [(c, c ^ k) for c in range(count)])
        pieces.append(piece)
    return pieces


def weights_kernel(shift_ref, u_ref, v_ref, out_ref):
    per_step, rows, cells = out_ref.shape
    first = pl.program_id(0) * per_step
    u_of = lax.broadcasted_iota(jnp.int32, (GRID, cells), 1) // GRID
    v_of = lax.broadcasted_iota(jnp.int32, (GRID, cells), 1) % GRID
    grid_row = lax.broadcasted_iota(jnp.int32, (GRID, cells), 0)
    spread_u = (u_of == grid_row).astype(jnp.bfloat16)
    spread_v = (v_of == grid_row).astype(jnp.bfloat16)
    dims = (((0,), (0,)), ((), ()))
    for k in range(per_step):
        shift = shift_ref[first + k]
        for part in range(rows // LANES):
            where = pl.ds(k * rows + part * LANES, LANES)
            u_part = pltpu.roll(u_ref[:, where].astype(jnp.float32), shift, 1).astype(jnp.bfloat16)
            v_part = pltpu.roll(v_ref[:, where].astype(jnp.float32), shift, 1).astype(jnp.bfloat16)
            u_wide = lax.dot_general(u_part, spread_u, dims, preferred_element_type=jnp.float32)
            v_wide = lax.dot_general(v_part, spread_v, dims, preferred_element_type=jnp.float32)
            out_ref[k, part * LANES : (part + 1) * LANES, :] = (u_wide * v_wide).astype(
                jnp.bfloat16
            )


def grid_weights(kern_u, kern_v, shifts):
    rows = SBLK * SBLK
    blocks = kern_u.shape[1] // rows
    per_step = 8
    spec = pl.BlockSpec((GRID, per_step * rows), lambda m, shift: (0, m))
    return pl.pallas_call(
        weights_kernel,
        grid_spec=pltpu.PrefetchScalarGridSpec(
            num_scalar_prefetch=1,
            grid=(blocks // per_step,),
            in_specs=[spec, spec],
            out_specs=pl.BlockSpec((per_step, rows, GRID * GRID), lambda m, shift: (m, 0, 0)),
        ),
        out_shape=jax.ShapeDtypeStruct((blocks, rows, GRID * GRID), jnp.bfloat16),
        compiler_params=pltpu.CompilerParams(vmem_limit_bytes=VMEM_LIMIT),
        cost_estimate=pl.CostEstimate(
            flops=2048 * blocks * rows * GRID, bytes_accessed=0, transcendentals=0
        ),
    )(shifts, kern_u, kern_v)


def correlate_kernel(
    scale, sources, parity, owned, slot_ref, me_ref, owner_ref, *refs
):
    early_refs, late_refs = refs[:sources], refs[sources : 2 * sources]
    weights_hbm, out_ref = refs[2 * sources : 2 * sources + 2]
    staged, spectra, vis, blocks_a, blocks_b, acc, weights_ref, weights_sem = refs[
        2 * sources + 2 :
    ]
    early_frames, source_stations, width = early_refs[0].shape
    late_frames = late_refs[0].shape[0]
    frames = early_frames + late_frames
    stations = sources * source_stations
    group = width // 2
    tiles, rows, cells = out_ref.shape
    block_rows = stations // SBLK
    pieces = LANES // SBLK
    strip = LANES // 2
    strip_blocks = strip // SBLK
    pitch = rows + 1
    unroll = 8
    span = 4
    owners = tiles // owned

    copy = pltpu.make_async_copy(weights_hbm, weights_ref, weights_sem)
    copy.start()
    acc[...] = jnp.zeros_like(acc)

    def turn(frame, source_refs, lanes, place):
        for k in range(sources):
            start = pl.multiple_of((me_ref[0] ^ k) * source_stations, source_stations)
            staged[pl.ds(start, source_stations), :] = source_refs[k][frame, :, lanes].astype(
                jnp.float32
            )
        flipped = staged[...].T
        for side in range(2):
            spectra[side, pl.ds(place * pitch, width), :] = flipped[
                :, side * LANES : (side + 1) * LANES
            ]

    def turn_early(frame, carry):
        turn(frame, early_refs, slice(None), frame)
        return carry

    def turn_late(frame, carry):
        turn(frame, late_refs, slice(parity * width, (parity + 1) * width), frame + early_frames)
        return carry

    lax.fori_loop(0, early_frames, turn_early, 0)
    lax.fori_loop(0, late_frames, turn_late, 0)

    lane_piece = lax.broadcasted_iota(jnp.int32, (16, LANES), 1) // SBLK
    masks = [(lane_piece & (1 << bit)) != 0 for bit in range(3)]

    for index in range(stations // strip):
        own_side = index * strip // LANES
        offset = index * strip % LANES
        sides = tuple(range(own_side, 2))

        def channels(step, carry):
            for inner in range(unroll):
                channel = step * unroll + inner
                real = [
                    spectra.at[s][pl.ds(channel, frames, stride=pitch), :] for s in range(2)
                ]
                imag = [
                    spectra.at[s][pl.ds(group + channel, frames, stride=pitch), :]
                    for s in range(2)
                ]
                right = jnp.concatenate(
                    [jnp.concatenate([real[s], imag[s]], axis=0) for s in sides], axis=1
                ).astype(jnp.bfloat16)
                own_real = real[own_side][:, offset : offset + strip]
                own_imag = imag[own_side][:, offset : offset + strip]
                left = jnp.concatenate(
                    [
                        jnp.concatenate([own_real, own_imag], axis=1),
                        jnp.concatenate([own_imag, -own_real], axis=1),
                    ],
                    axis=0,
                ).astype(jnp.bfloat16)
                product = lax.dot_general(
                    left, right, (((0,), (0,)), ((), ())), preferred_element_type=jnp.float32
                )
                for part in range(2):
                    for place, side in enumerate(sides):
                        vis.at[side][pl.ds(part * group + channel, strip, stride=pitch), :] = (
                            product[
                                part * strip : (part + 1) * strip,
                                place * LANES : (place + 1) * LANES,
                            ]
                        )
            return carry

        lax.fori_loop(0, group // unroll, channels, 0)
        if index == 0:
            copy.wait()

        def rearrange(step, tile, target):
            side = own_side + step // strip_blocks
            local = step % strip_blocks
            row = pl.multiple_of(tile * 16, 16)
            for upper in range(2):
                turned = []
                for a in range(pieces):
                    start = (local * SBLK + upper * pieces + a) * pitch + row
                    value = vis[side, pl.ds(start, 16), :]
                    if a:
                        value = pltpu.roll(value, a * SBLK, 1)
                    turned.append(value)
                for bit in range(3):
                    turned = [
                        jnp.where(masks[bit], turned[(x + (1 << bit)) % pieces], turned[x])
                        for x in range(pieces)
                    ]
                for piece in range(pieces):
                    target[piece, pl.ds(row, 16), upper * LANES : (upper + 1) * LANES] = turned[
                        -piece % pieces
                    ].astype(jnp.bfloat16)

        steps = strip_blocks * len(sides)
        per_piece = rows // 16 // pieces

        def first(tile, carry):
            rearrange(0, tile, blocks_a)
            return carry

        lax.fori_loop(0, rows // 16, first, 0)

        def pieces_step(step, begin, current, following, gridding):
            p = index * strip_blocks + step % strip_blocks
            side = own_side + step // strip_blocks
            next_step = jnp.minimum(step + 1, steps - 1)
            for inner in range(span):
                piece = begin + inner
                if gridding:
                    q = side * pieces + piece
                    valid = q > p
                    m = jnp.where(valid, p * (2 * block_rows - p - 1) // 2 + q - p - 1, 0)
                    slot = jnp.where(valid, slot_ref[m], tiles)
                    product = jnp.dot(
                        current[piece], weights_ref[m], preferred_element_type=jnp.float32
                    )
                for tile in range(per_piece):
                    rearrange(next_step, piece * per_piece + tile, following)
                if gridding:
                    acc[slot] += product

        for place, side in enumerate(sides):
            lower = side == own_side and offset >= span * SBLK

            def pair_step(pair, carry):
                for odd, (current, following) in enumerate(
                    ((blocks_a, blocks_b), (blocks_b, blocks_a))
                ):
                    step = place * strip_blocks + 2 * pair + odd

                    def some_pieces(turn_index, inner):
                        pieces_step(step, turn_index * span, current, following, True)
                        return inner

                    if lower:
                        pieces_step(step, 0, current, following, False)
                        pieces_step(step, span, current, following, True)
                    else:
                        lax.fori_loop(0, pieces // span, some_pieces, 0)
                return carry

            lax.fori_loop(0, strip_blocks // 2, pair_step, 0)

    for k in range(owners):
        first_tile = (owner_ref[0] + k) % owners * owned
        for tile in range(owned):
            out_ref[k * owned + tile] = (acc[first_tile + tile] * scale).astype(out_ref.dtype)


def gridded(early, late, parity, weights, slot_of_block, me, owner, tile_count, total_frames, owned):
    sources = len(early)
    early_frames, source_stations, width = early[0].shape
    frames = early_frames + late[0].shape[0]
    stations = sources * source_stations
    cells = GRID * GRID
    pitch = width + 1
    whole = pl.BlockSpec(memory_space=pltpu.VMEM)
    scalars = pl.BlockSpec(memory_space=pltpu.SMEM)
    block = pltpu.VMEM((LANES // SBLK, width, SBLK * SBLK), jnp.bfloat16)
    return pl.pallas_call(
        functools.partial(
            correlate_kernel, 1.0 / math.sqrt(total_frames), sources, parity, owned
        ),
        in_specs=[scalars] * 3 + [whole] * (2 * sources) + [pl.BlockSpec(memory_space=pl.ANY)],
        out_specs=whole,
        out_shape=jax.ShapeDtypeStruct((tile_count, width, cells), jnp.bfloat16),
        scratch_shapes=[
            pltpu.VMEM((stations, width), jnp.float32),
            pltpu.VMEM((2, -(-frames * pitch // 8) * 8, LANES), jnp.float32),
            pltpu.VMEM((2, LANES // 2 * pitch, LANES), jnp.float32),
            block,
            block,
            pltpu.VMEM((tile_count + 1, width, cells), jnp.float32),
            pltpu.VMEM(weights.shape, weights.dtype),
            pltpu.SemaphoreType.DMA,
        ],
        compiler_params=pltpu.CompilerParams(vmem_limit_bytes=VMEM_LIMIT),
        cost_estimate=pl.CostEstimate(
            flops=48 * weights.size * width,
            bytes_accessed=2 * weights.size,
            transcendentals=0,
        ),
    )(slot_of_block, me, owner, *early, *late, weights)


def body(samples, taps, block_tile, tile_slots, kern_u, kern_v):
    station_count, frame_count, length = samples.shape
    chan_size = lax.axis_size("chan")
    tm_size = lax.axis_size("tm")
    half = length // 2
    history = passed_along(samples[:, frame_count - HISTORY :], "tm", 1)
    me = lax.axis_index("chan").astype(jnp.int32).reshape(1)
    tables = [jnp.asarray(table) for table in dft_tables(length, chan_size)]
    dft_scale = 1.0 / math.sqrt(length)

    tile_count = tile_slots.shape[0]
    slot_ids = jnp.arange(tile_count, dtype=jnp.int32)
    tile_match = block_tile[:, None] == tile_slots[None, :]
    slot_of_block = jnp.sum(jnp.where(tile_match, slot_ids[None, :], 0), axis=1).astype(jnp.int32)
    pairs = block_pairs(station_count * chan_size // SBLK)
    pieces = LANES // SBLK
    shifts = jnp.asarray((pairs[:, 1] % pieces) * SBLK, jnp.int32)
    weights = grid_weights(kern_u, kern_v, shifts)

    def spectra_of(rows_in, parity):
        rows_in = rows_in.reshape(rows_in.shape[0] * station_count, half)
        return dft(rows_in, tables[parity], chan_size, dft_scale, me)

    late_rows = filtered_halves(samples, None, taps)
    late_blocks = jnp.concatenate([spectra_of(late_rows[0], 0), spectra_of(late_rows[1], 1)], axis=2)
    late = exchanged(late_blocks, (frame_count - HISTORY, station_count, late_blocks.shape[2]))
    early_taps, weights = lax.optimization_barrier((taps, weights))
    early_rows = filtered_halves(samples, history, early_taps)
    early_blocks = [spectra_of(early_rows[parity], parity) for parity in range(2)]
    even_weights, early_blocks[1] = lax.optimization_barrier((weights, early_blocks[1]))

    owner = lax.axis_index("tm").astype(jnp.int32).reshape(1)
    owned = tile_count // tm_size
    grids = []
    for parity in range(2):
        blocks = early_blocks[parity]
        early = exchanged(blocks, (HISTORY, station_count, blocks.shape[2]))
        partial_grid = gridded(
            early,
            late,
            parity,
            even_weights if parity == 0 else weights,
            slot_of_block,
            me,
            owner,
            tile_count,
            frame_count * tm_size,
            owned,
        )
        total = partial_grid[:owned].astype(jnp.float32)
        for k in range(1, tm_size):
            piece = lax.ppermute(
                partial_grid[k * owned : (k + 1) * owned],
                "tm",
                [(z, (z + k) % tm_size) for z in range(tm_size)],
            )
            total = total + piece.astype(jnp.float32)
        _, rows, cells = total.shape
        total = total.reshape(owned, 2, rows // 2, cells).transpose(0, 2, 1, 3)
        grids.append(total[:, :, None])
    uv_grid = jnp.concatenate(grids, axis=2)
    return uv_grid.reshape(uv_grid.shape[0], -1, 2, uv_grid.shape[-1])


def solution(mesh):
    placed = (P("chan", "tm", None), P(), P(), P(), P(), P())
    return jax.shard_map(
        body, mesh=mesh, in_specs=placed, out_specs=P("tm", "chan", None, None), check_vma=False
    )
```

```python
import functools
import math

import jax
import jax.numpy as jnp
import numpy as np
from jax import lax
from jax.experimental import pallas as pl
from jax.experimental.pallas import tpu as pltpu
from jax.sharding import PartitionSpec as P

SBLK = 16
GRID = 16
LANES = 128
HISTORY = 16
VMEM_LIMIT = 60 * 1024 * 1024


def passed_along(value, axis, steps):
    count = lax.axis_size(axis)
    leading, last = (max(0, -steps), min(count, count - steps))
    return lax.ppermute(value, axis, [(source, source + steps) for source in range(leading, last)])


def block_pairs(block_total):
    pairs = [(p, q) for p in range(block_total) for q in range(p + 1, block_total)]
    return np.array(pairs, dtype=np.int32)


def dft_tables(length, chan_size):
    half = length // 2
    channels = length // 2
    width = channels // chan_size // 2
    positions = np.arange(half, dtype=np.int64)[:, None, None]
    tables = []
    for parity in range(2):
        chans = (
            np.arange(chan_size, dtype=np.int64)[:, None] * 2 * width
            + 2 * np.arange(width, dtype=np.int64)[None, :]
            + parity
        )[None]
        angle = ((positions * chans) % length).astype(np.float64) * (2.0 * math.pi / length)
        table = np.stack([np.cos(angle), -np.sin(angle)], axis=2)
        table = table.reshape(half, chan_size, 2 * width).transpose(1, 0, 2)
        tables.append(table.astype(jnp.bfloat16))
    return np.stack(tables)


def filter_kernel(early, *refs):
    if early:
        hist_lo, hist_hi, lo_ref, hi_ref, taps_lo_ref, taps_hi_ref, even_ref, odd_ref, wide = refs
        parts = ((hist_lo, lo_ref), (hist_hi, hi_ref))
    else:
        lo_ref, hi_ref, taps_lo_ref, taps_hi_ref, even_ref, odd_ref, wide = refs
        parts = ((lo_ref,), (hi_ref,))
    frames, stations, cols = even_ref.shape
    tap_count = taps_lo_ref.shape[0]
    for side, sources in enumerate(parts):
        if early:
            wide[side, :HISTORY] = jnp.swapaxes(sources[0][...].astype(jnp.float32), 0, 1)
            whole = jnp.swapaxes(sources[1][...].astype(jnp.float32), 0, 1)
            wide[side, HISTORY:] = whole[:frames]
        else:
            wide[side] = jnp.swapaxes(sources[0][...].astype(jnp.float32), 0, 1)
    span = 4
    rows = 16
    for lane in range(0, cols, LANES):
        lanes = slice(lane, lane + LANES)

        def step(index, carry):
            station = pl.multiple_of((index % (stations // rows)) * rows, rows)
            frame = (index // (stations // rows)) * span
            sums = []
            for side, taps_ref in enumerate((taps_lo_ref, taps_hi_ref)):
                values = [
                    wide[side, frame + HISTORY - (tap_count - 1) + k, pl.ds(station, rows), lanes]
                    for k in range(span + tap_count - 1)
                ]
                accs = [jnp.zeros((rows, LANES), jnp.float32) for _ in range(span)]
                for tap in range(tap_count):
                    weight = taps_ref[tap : tap + 1, lanes]
                    for b in range(span):
                        accs[b] = accs[b] + weight * values[b + tap_count - 1 - tap]
                sums.append(accs)
            for b in range(span):
                even_ref[frame + b, pl.ds(station, rows), lanes] = (
                    sums[0][b] + sums[1][b]
                ).astype(jnp.bfloat16)
                odd_ref[frame + b, pl.ds(station, rows), lanes] = (
                    sums[0][b] - sums[1][b]
                ).astype(jnp.bfloat16)
            return carry

        lax.fori_loop(0, (stations // rows) * (frames // span), step, 0)


def filtered_halves(samples, history, taps, part=0, parts=1):
    stations, all_frames, length = samples.shape
    stations = stations // parts
    early = history is not None
    frames = HISTORY if early else all_frames - HISTORY
    tap_count = taps.shape[0]
    half = length // 2
    cols = 256
    steps = half // cols
    lo = lambda j: (0, 0, j)
    hi = lambda j: (0, 0, j + steps)
    out = jax.ShapeDtypeStruct((frames, stations, half), jnp.bfloat16)
    out_spec = pl.BlockSpec((frames, stations, cols), lo)
    operands = [samples, samples, taps, taps]
    specs = [
        pl.BlockSpec((stations, all_frames, cols), lambda j: (part, 0, j)),
        pl.BlockSpec((stations, all_frames, cols), lambda j: (part, 0, j + steps)),
        pl.BlockSpec((tap_count, cols), lambda j: (0, j)),
        pl.BlockSpec((tap_count, cols), lambda j: (0, j + steps)),
    ]
    if early:
        operands = [history, history] + operands
        specs = [
            pl.BlockSpec((stations, HISTORY, cols), lo),
            pl.BlockSpec((stations, HISTORY, cols), hi),
        ] + specs
    return pl.pallas_call(
        functools.partial(filter_kernel, early),
        grid=(steps,),
        in_specs=specs,
        out_specs=[out_spec, out_spec],
        out_shape=[out, out],
        scratch_shapes=[pltpu.VMEM((2, HISTORY + frames, stations, cols), jnp.float32)],
        compiler_params=pltpu.CompilerParams(vmem_limit_bytes=VMEM_LIMIT),
        cost_estimate=pl.CostEstimate(
            flops=640 * tap_count * stations * frames * length,
            bytes_accessed=4 * samples.size,
            transcendentals=0,
        ),
    )(*operands)


def dft_kernel(scale, me_ref, even_ref, odd_ref, table_ref, out_ref):
    for parity, rows_ref in enumerate((even_ref, odd_ref)):

        @pl.when(pl.program_id(1) == parity)
        def _():
            out_ref[0] = (
                jnp.dot(rows_ref[...], table_ref[0, 0], preferred_element_type=jnp.float32) * scale
            ).astype(jnp.bfloat16)


def dft(even, odd, tables, scale, me):
    row_count, depth = even.shape
    _, chan_size, _, width = tables.shape
    rows = pl.BlockSpec((row_count, depth), lambda k, parity, me: (0, 0))
    return pl.pallas_call(
        functools.partial(dft_kernel, scale),
        grid_spec=pltpu.PrefetchScalarGridSpec(
            num_scalar_prefetch=1,
            grid=(chan_size, 2),
            in_specs=[
                rows,
                rows,
                pl.BlockSpec((1, 1, depth, width), lambda k, parity, me: (parity, me[0] ^ k, 0, 0)),
            ],
            out_specs=pl.BlockSpec((1, row_count, width), lambda k, parity, me: (k, 0, parity)),
        ),
        out_shape=jax.ShapeDtypeStruct((chan_size, row_count, 2 * width), jnp.bfloat16),
        compiler_params=pltpu.CompilerParams(vmem_limit_bytes=VMEM_LIMIT),
        cost_estimate=pl.CostEstimate(
            flops=2 * row_count * tables.size,
            bytes_accessed=2 * (2 * even.size + tables.size + row_count * 2 * chan_size * width),
            transcendentals=0,
        ),
    )(me, even, odd, tables)


def exchanged(blocks, shape):
    count = blocks.shape[0]
    pieces = []
    for k in range(count):
        piece = blocks[k].reshape(shape)
        if k:
            piece = lax.ppermute(piece, "chan", [(c, c ^ k) for c in range(count)])
        pieces.append(piece)
    return pieces


def weights_kernel(shift_ref, u_ref, v_ref, out_ref):
    per_step, rows, cells = out_ref.shape
    first = pl.program_id(0) * per_step
    u_of = lax.broadcasted_iota(jnp.int32, (GRID, cells), 1) // GRID
    v_of = lax.broadcasted_iota(jnp.int32, (GRID, cells), 1) % GRID
    grid_row = lax.broadcasted_iota(jnp.int32, (GRID, cells), 0)
    spread_u = (u_of == grid_row).astype(jnp.bfloat16)
    spread_v = (v_of == grid_row).astype(jnp.bfloat16)
    dims = (((0,), (0,)), ((), ()))
    for k in range(per_step):
        shift = shift_ref[first + k]
        for part in range(rows // LANES):
            where = pl.ds(k * rows + part * LANES, LANES)
            u_part = pltpu.roll(u_ref[:, where].astype(jnp.float32), shift, 1).astype(jnp.bfloat16)
            v_part = pltpu.roll(v_ref[:, where].astype(jnp.float32), shift, 1).astype(jnp.bfloat16)
            u_wide = lax.dot_general(u_part, spread_u, dims, preferred_element_type=jnp.float32)
            v_wide = lax.dot_general(v_part, spread_v, dims, preferred_element_type=jnp.float32)
            out_ref[k, part * LANES : (part + 1) * LANES, :] = (u_wide * v_wide).astype(
                jnp.bfloat16
            )


def grid_weights(kern_u, kern_v, shifts):
    rows = SBLK * SBLK
    blocks = kern_u.shape[1] // rows
    per_step = 8
    spec = pl.BlockSpec((GRID, per_step * rows), lambda m, shift: (0, m))
    return pl.pallas_call(
        weights_kernel,
        grid_spec=pltpu.PrefetchScalarGridSpec(
            num_scalar_prefetch=1,
            grid=(blocks // per_step,),
            in_specs=[spec, spec],
            out_specs=pl.BlockSpec((per_step, rows, GRID * GRID), lambda m, shift: (m, 0, 0)),
        ),
        out_shape=jax.ShapeDtypeStruct((blocks, rows, GRID * GRID), jnp.bfloat16),
        compiler_params=pltpu.CompilerParams(vmem_limit_bytes=VMEM_LIMIT),
        cost_estimate=pl.CostEstimate(
            flops=2048 * blocks * rows * GRID, bytes_accessed=0, transcendentals=0
        ),
    )(shifts, kern_u, kern_v)


def correlate_kernel(
    scale, sources, parts, parity, owned, slot_ref, me_ref, owner_ref, *refs
):
    early_count = parts * sources
    early_refs, late_refs = refs[:early_count], refs[early_count : early_count + sources]
    refs = refs[early_count + sources :]
    weights_hbm, out_ref = refs[:2]
    staged, spectra, vis, blocks_a, blocks_b, acc, weights_ref, weights_sem = refs[2:]
    early_frames = early_refs[0].shape[0]
    late_frames, source_stations, both = late_refs[0].shape
    width = both // 2
    lanes = slice(parity * width, (parity + 1) * width)
    frames = early_frames + late_frames
    stations = sources * source_stations
    group = width // 2
    tiles, rows, cells = out_ref.shape
    block_rows = stations // SBLK
    pieces = LANES // SBLK
    strip = LANES // 2
    strip_blocks = strip // SBLK
    pitch = rows + 1
    unroll = 8
    span = 4
    owners = tiles // owned

    copy = pltpu.make_async_copy(weights_hbm, weights_ref, weights_sem)
    copy.start()
    acc[...] = jnp.zeros_like(acc)

    def turn(frame, source_refs, place):
        count = len(source_refs) // sources
        rows_each = source_stations // count
        for part in range(count):
            for k in range(sources):
                start = (me_ref[0] ^ k) * source_stations + part * rows_each
                staged[pl.ds(pl.multiple_of(start, rows_each), rows_each), :] = source_refs[
                    part * sources + k
                ][frame, :, lanes].astype(jnp.float32)
        flipped = staged[...].T
        for side in range(2):
            spectra[side, pl.ds(place * pitch, width), :] = flipped[
                :, side * LANES : (side + 1) * LANES
            ]

    def turn_early(frame, carry):
        turn(frame, early_refs, frame)
        return carry

    def turn_late(frame, carry):
        turn(frame, late_refs, frame + early_frames)
        return carry

    lax.fori_loop(0, early_frames, turn_early, 0)
    lax.fori_loop(0, late_frames, turn_late, 0)

    lane_piece = lax.broadcasted_iota(jnp.int32, (16, LANES), 1) // SBLK
    masks = [(lane_piece & (1 << bit)) != 0 for bit in range(3)]

    for index in range(stations // strip):
        own_side = index * strip // LANES
        offset = index * strip % LANES
        sides = tuple(range(own_side, 2))

        def channels(step, carry):
            for inner in range(unroll):
                channel = step * unroll + inner
                real = [
                    spectra.at[s][pl.ds(channel, frames, stride=pitch), :] for s in range(2)
                ]
                imag = [
                    spectra.at[s][pl.ds(group + channel, frames, stride=pitch), :]
                    for s in range(2)
                ]
                right = jnp.concatenate(
                    [jnp.concatenate([real[s], imag[s]], axis=0) for s in sides], axis=1
                ).astype(jnp.bfloat16)
                own_real = real[own_side][:, offset : offset + strip]
                own_imag = imag[own_side][:, offset : offset + strip]
                left = jnp.concatenate(
                    [
                        jnp.concatenate([own_real, own_imag], axis=1),
                        jnp.concatenate([own_imag, -own_real], axis=1),
                    ],
                    axis=0,
                ).astype(jnp.bfloat16)
                product = lax.dot_general(
                    left, right, (((0,), (0,)), ((), ())), preferred_element_type=jnp.float32
                )
                for part in range(2):
                    for place, side in enumerate(sides):
                        vis.at[side][pl.ds(part * group + channel, strip, stride=pitch), :] = (
                            product[
                                part * strip : (part + 1) * strip,
                                place * LANES : (place + 1) * LANES,
                            ]
                        )
            return carry

        lax.fori_loop(0, group // unroll, channels, 0)
        if index == 0:
            copy.wait()

        def rearrange(step, tile, target):
            side = own_side + step // strip_blocks
            local = step % strip_blocks
            row = pl.multiple_of(tile * 16, 16)
            for upper in range(2):
                turned = []
                for a in range(pieces):
                    start = (local * SBLK + upper * pieces + a) * pitch + row
                    value = vis[side, pl.ds(start, 16), :]
                    if a:
                        value = pltpu.roll(value, a * SBLK, 1)
                    turned.append(value)
                for bit in range(3):
                    turned = [
                        jnp.where(masks[bit], turned[(x + (1 << bit)) % pieces], turned[x])
                        for x in range(pieces)
                    ]
                for piece in range(pieces):
                    target[piece, pl.ds(row, 16), upper * LANES : (upper + 1) * LANES] = turned[
                        -piece % pieces
                    ].astype(jnp.bfloat16)

        steps = strip_blocks * len(sides)
        per_piece = rows // 16 // pieces

        def first(tile, carry):
            rearrange(0, tile, blocks_a)
            return carry

        lax.fori_loop(0, rows // 16, first, 0)

        def pieces_step(step, begin, current, following, gridding):
            p = index * strip_blocks + step % strip_blocks
            side = own_side + step // strip_blocks
            next_step = jnp.minimum(step + 1, steps - 1)
            for inner in range(span):
                piece = begin + inner
                if gridding:
                    q = side * pieces + piece
                    valid = q > p
                    m = jnp.where(valid, p * (2 * block_rows - p - 1) // 2 + q - p - 1, 0)
                    slot = jnp.where(valid, slot_ref[m], tiles)
                    product = jnp.dot(
                        current[piece], weights_ref[m], preferred_element_type=jnp.float32
                    )
                for tile in range(per_piece):
                    rearrange(next_step, piece * per_piece + tile, following)
                if gridding:
                    acc[slot] += product

        for place, side in enumerate(sides):
            lower = side == own_side and offset >= span * SBLK

            def pair_step(pair, carry):
                for odd, (current, following) in enumerate(
                    ((blocks_a, blocks_b), (blocks_b, blocks_a))
                ):
                    step = place * strip_blocks + 2 * pair + odd

                    def some_pieces(turn_index, inner):
                        pieces_step(step, turn_index * span, current, following, True)
                        return inner

                    if lower:
                        pieces_step(step, 0, current, following, False)
                        pieces_step(step, span, current, following, True)
                    else:
                        lax.fori_loop(0, pieces // span, some_pieces, 0)
                return carry

            lax.fori_loop(0, strip_blocks // 2, pair_step, 0)

    for k in range(owners):
        first_tile = (owner_ref[0] + k) % owners * owned
        for tile in range(owned):
            out_ref[k * owned + tile] = (acc[first_tile + tile] * scale).astype(out_ref.dtype)


def gridded(early, late, parity, weights, slot_of_block, me, owner, tile_count, total_frames, owned):
    sources = len(late)
    parts = len(early) // sources
    late_frames, source_stations, both = late[0].shape
    width = both // 2
    frames = early[0].shape[0] + late_frames
    stations = sources * source_stations
    cells = GRID * GRID
    pitch = width + 1
    whole = pl.BlockSpec(memory_space=pltpu.VMEM)
    scalars = pl.BlockSpec(memory_space=pltpu.SMEM)
    block = pltpu.VMEM((LANES // SBLK, width, SBLK * SBLK), jnp.bfloat16)
    return pl.pallas_call(
        functools.partial(
            correlate_kernel, 1.0 / math.sqrt(total_frames), sources, parts, parity, owned
        ),
        in_specs=[scalars] * 3 + [whole] * (len(early) + sources) + [pl.BlockSpec(memory_space=pl.ANY)],
        out_specs=whole,
        out_shape=jax.ShapeDtypeStruct((tile_count, width, cells), jnp.bfloat16),
        scratch_shapes=[
            pltpu.VMEM((stations, width), jnp.float32),
            pltpu.VMEM((2, -(-frames * pitch // 8) * 8, LANES), jnp.float32),
            pltpu.VMEM((2, LANES // 2 * pitch, LANES), jnp.float32),
            block,
            block,
            pltpu.VMEM((tile_count + 1, width, cells), jnp.float32),
            pltpu.VMEM(weights.shape, weights.dtype),
            pltpu.SemaphoreType.DMA,
        ],
        compiler_params=pltpu.CompilerParams(vmem_limit_bytes=VMEM_LIMIT),
        cost_estimate=pl.CostEstimate(
            flops=48 * weights.size * width,
            bytes_accessed=2 * weights.size,
            transcendentals=0,
        ),
    )(slot_of_block, me, owner, *early, *late, weights)


def body(samples, taps, block_tile, tile_slots, kern_u, kern_v):
    station_count, frame_count, length = samples.shape
    chan_size = lax.axis_size("chan")
    tm_size = lax.axis_size("tm")
    half = length // 2
    parts = 2 if station_count % 32 == 0 else 1
    part_stations = station_count // parts
    histories = []
    for part in range(parts):
        tail = samples[part * part_stations : (part + 1) * part_stations, frame_count - HISTORY :]
        if part:
            tail, histories[-1] = lax.optimization_barrier((tail, histories[-1]))
        histories.append(passed_along(tail, "tm", 1))
    me = lax.axis_index("chan").astype(jnp.int32).reshape(1)
    tables = jnp.asarray(dft_tables(length, chan_size))
    dft_scale = 1.0 / math.sqrt(length)

    tile_count = tile_slots.shape[0]
    slot_ids = jnp.arange(tile_count, dtype=jnp.int32)
    tile_match = block_tile[:, None] == tile_slots[None, :]
    slot_of_block = jnp.sum(jnp.where(tile_match, slot_ids[None, :], 0), axis=1).astype(jnp.int32)
    pairs = block_pairs(station_count * chan_size // SBLK)
    pieces = LANES // SBLK
    shifts = jnp.asarray((pairs[:, 1] % pieces) * SBLK, jnp.int32)
    weights = grid_weights(kern_u, kern_v, shifts)

    def exchanged_spectra(rows):
        frames, stations, _ = rows[0].shape
        even, odd = (half_rows.reshape(frames * stations, half) for half_rows in rows)
        blocks = dft(even, odd, tables, dft_scale, me)
        return exchanged(blocks, (frames, stations, blocks.shape[2]))

    late = exchanged_spectra(filtered_halves(samples, None, taps))
    early_taps = taps
    early = []
    for part in range(parts):
        if part == parts - 1:
            early_taps, weights = lax.optimization_barrier((taps, weights))
        early += exchanged_spectra(
            filtered_halves(samples, histories[part], early_taps, part, parts)
        )

    owner = lax.axis_index("tm").astype(jnp.int32).reshape(1)
    owned = tile_count // tm_size
    grids = []
    for parity in range(2):
        partial_grid = gridded(
            early,
            late,
            parity,
            weights,
            slot_of_block,
            me,
            owner,
            tile_count,
            frame_count * tm_size,
            owned,
        )
        total = partial_grid[:owned].astype(jnp.float32)
        for k in range(1, tm_size):
            piece = lax.ppermute(
                partial_grid[k * owned : (k + 1) * owned],
                "tm",
                [(z, (z + k) % tm_size) for z in range(tm_size)],
            )
            total = total + piece.astype(jnp.float32)
        _, rows, cells = total.shape
        total = total.reshape(owned, 2, rows // 2, cells).transpose(0, 2, 1, 3)
        grids.append(total[:, :, None])
    uv_grid = jnp.concatenate(grids, axis=2)
    return uv_grid.reshape(uv_grid.shape[0], -1, 2, uv_grid.shape[-1])


def solution(mesh):
    placed = (P("chan", "tm", None), P(), P(), P(), P(), P())
    return jax.shard_map(
        body, mesh=mesh, in_specs=placed, out_specs=P("tm", "chan", None, None), check_vma=False
    )
```
